256 devices in a mesh: seq: 64 (over z, y, core), ch: 4 (over x).
Axes of the slice: x: 4, y: 4, z: 8, core: 2. Of those that a mesh axis runs over, the one named last changes fastest.
Arguments:
- value_in: bfloat16 [4, 512, 8192], P('ch', None, 'seq'), may hold values from -6 to 6
- gate_in: bfloat16 [4, 512, 8192], P('ch', None, 'seq'), may hold values from -6 to 6
- grad_out: bfloat16 [4, 512, 8192], P('ch', None, 'seq'), may hold values from -6 to 6
- filters: float32 [512, 8192], P('seq'), may hold values from -2 to 2
- genome_lengths: int32 [4], replicated, may hold values from 512 to 4096, as said below
Outputs:
- gated_out: bfloat16 [4, 512, 8192], P('ch', None, 'seq')
- grad_value: bfloat16 [4, 512, 8192], P('ch', None, 'seq')
- grad_gate: bfloat16 [4, 512, 8192], P('ch', None, 'seq')
- grad_filters: float32 [512, 8192], P('seq', 'ch')
The draws below stay inside these ranges and needn't reach their ends.
Inputs may be any that keep to these rules, and one draw needn't show every extreme that they name: `genome_lengths`: the lengths are multiples of 512, sum to 8192, and one of them is exactly 4096.
All inputs are finite; a program needn't handle non-finite values.
Results may differ from the reference program's by a relative error of at most 0.012.
Values may be sent and summed in bfloat16 or wider, within the bound.
A program may use at most 128 MiB of HBM per device.

```python
import math
import jax
import jax.numpy as jnp
from jax import lax

GS = 4
NF = 512
NBLK = 16
NGEN = 4
TOKENS = 8192


def draw_filters(key, part):
    key = jax.random.fold_in(key, 11)
    pick_key, rate_key, noise_key = jax.random.split(key, 3)
    positions = jnp.arange(TOKENS, dtype=jnp.float32)[None, :]
    slow_share = 0.5
    slow_flag = (jax.random.uniform(pick_key, (NF, 1)) < slow_share).astype(jnp.float32)
    mixing = jax.random.uniform(rate_key, (NF, 1))
    slow_rate = jnp.exp(math.log(0.1 / TOKENS) + mixing * math.log(20.0))
    fast_rate = jnp.exp(math.log(1.0 / 50.0) + mixing * math.log(50.0 / 30.0))
    decay_rate = slow_flag * slow_rate + (1.0 - slow_flag) * fast_rate
    normalizer = jnp.sqrt(jnp.expm1(-2.0 * decay_rate) / jnp.expm1(-2.0 * decay_rate * TOKENS))
    noise_draw = jax.random.truncated_normal(noise_key, -4.0, 4.0, (NF, TOKENS))
    return (noise_draw * jnp.exp(-decay_rate * positions) * normalizer).astype(jnp.float32)


def draw_genome_lengths(key, part):
    key = jax.random.fold_in(key, 5)
    order_key, place_key = jax.random.split(key)
    remainder = NBLK - NBLK // 2
    cut_points = jnp.sort(jax.random.permutation(order_key, remainder - 1)[:NGEN - 2] + 1).astype(jnp.int32)
    cut_edges = jnp.concatenate([jnp.zeros((1,), jnp.int32), cut_points, jnp.full((1,), remainder, jnp.int32)])
    pieces = cut_edges[1:] - cut_edges[:-1]
    extended = jnp.concatenate([pieces, jnp.zeros((1,), jnp.int32)])
    indices = jnp.arange(NGEN, dtype=jnp.int32)
    largest_spot = jax.random.randint(place_key, (), 0, NGEN)
    before_spot = extended[jnp.minimum(indices, NGEN - 2)]
    after_spot = extended[jnp.maximum(indices - 1, 0)]
    counts = jnp.where(indices == largest_spot, NBLK // 2, jnp.where(indices < largest_spot, before_spot, after_spot))
    return (counts * (TOKENS // NBLK)).astype(jnp.int32)


def levels(rng, extent, cuts, smallest, high):
    factor_of = 1.0
    for axis_at, shards_of in cuts:
        steps = jax.random.uniform(jax.random.fold_in(jax.random.fold_in(rng, 6), axis_at), (shards_of,), jnp.float32, smallest / len(cuts), high / len(cuts))
        factor_of = factor_of * jnp.repeat(jnp.exp(steps), extent[axis_at] // shards_of).reshape((-1,) + (1,) * (len(extent) - 1 - axis_at))
    return factor_of


def bell_draw(stream_key, shape, scale, reach, shards=(), held_as=jnp.bfloat16):
    loudness = levels(stream_key, shape, shards, -0.22, 0.18) if shards else 1.0
    values = jax.random.normal(stream_key, shape, jnp.float32) * scale * loudness
    return jnp.minimum(jnp.maximum(values, -reach), reach).astype(held_as)


def setup_inputs(seed: int = 0) -> dict:
    keys = jax.random.split(jax.random.key(seed), 6)
    return {
        "value_in": bell_draw(keys[0], (GS, NF, TOKENS), 1.0, 6.0, ((0, 4), (2, 64))),
        "gate_in": bell_draw(keys[1], (GS, NF, TOKENS), 1.0, 6.0, ((0, 4), (2, 64))),
        "grad_out": bell_draw(keys[2], (GS, NF, TOKENS), 1.0, 6.0, ((0, 4), (2, 64))),
        "filters": draw_filters(jax.random.fold_in(keys[5], 71), 0),
        "genome_lengths": draw_genome_lengths(jax.random.fold_in(keys[5], 71), 0),
    }


def genome_conv(values, kernel, genome_lengths):
    length = values.shape[-1]
    genome_ends = jnp.cumsum(genome_lengths).astype(jnp.int32)
    genome_starts = genome_ends - genome_lengths.astype(jnp.int32)
    positions = jnp.arange(length, dtype=jnp.int32)
    kernel_spectrum = jnp.fft.rfft(kernel, n=2 * length)
    summed = jnp.zeros_like(values)
    for genome in range(NGEN):
        inside = ((positions >= genome_starts[genome]) & (positions < genome_ends[genome])).astype(values.dtype)
        spectrum = jnp.fft.rfft(values * inside, n=2 * length)
        waveform = jnp.fft.irfft(spectrum * kernel_spectrum, n=2 * length)[..., :length]
        summed = summed + waveform * inside
    return summed

def reference(value_in, gate_in, grad_out, filters, genome_lengths):
    slab = min(64, NF)
    slab_count = NF // slab

    def to_slabs(array):
        return jnp.moveaxis(array.reshape(GS, slab_count, slab, TOKENS), 1, 0)

    def from_slabs(array):
        return jnp.moveaxis(array, 0, 1).reshape(GS, NF, TOKENS)

    def per_slab(operands):
        values, gates, cotangent, kernel = operands
        conv_full, pullback = jax.vjp(lambda left, right: genome_conv(left, right, genome_lengths), values.astype(jnp.float32), kernel)
        conv_low = lax.optimization_barrier(conv_full.astype(jnp.bfloat16))
        conv_wide = conv_low.astype(jnp.float32)
        gates_wide = gates.astype(jnp.float32)
        cot_wide = cotangent.astype(jnp.float32)
        gated = (gates_wide * conv_wide).astype(jnp.bfloat16)
        grad_conv = lax.optimization_barrier((cot_wide * gates_wide).astype(jnp.bfloat16))
        grad_gate = (cot_wide * conv_wide).astype(jnp.bfloat16)
        grad_values, grad_kernel = pullback(grad_conv.astype(jnp.float32))
        return (gated, grad_values.astype(jnp.bfloat16), grad_gate, grad_kernel)
    outputs = lax.map(per_slab, (to_slabs(value_in), to_slabs(gate_in), to_slabs(grad_out), filters.reshape(slab_count, slab, TOKENS)))
    return (from_slabs(outputs[0]), from_slabs(outputs[1]), from_slabs(outputs[2]), outputs[3].reshape(NF, TOKENS))
```

```python
import functools

import jax
import jax.numpy as jnp
from jax import lax
from jax.experimental import pallas as pl
from jax.experimental.pallas import tpu as pltpu
from jax.sharding import PartitionSpec as P

MESH = pl.DeviceIdType.MESH
F32 = jnp.float32
BF16 = jnp.bfloat16

PEERS = 64
NFL = 8
TOK = 128
ROWS = 32
LAGS = 16
SPAN = 4096


def anti_identity(n, dtype):
    row = lax.broadcasted_iota(jnp.int32, (n, n), 0)
    col = lax.broadcasted_iota(jnp.int32, (n, n), 1)
    return (row + col == n - 1).astype(dtype)


def partner(k, seq):
    z, y, c = seq >> 3, (seq >> 1) & 3, seq & 1
    dz, dy, dc = (3 * k) & 7, ((k >> 3) + k) & 3, k >> 5
    return (((((z + dz) & 7) << 2) + ((y + dy) & 3)) << 1) + (c ^ dc)


def kernel(
    lengths, value, gate, cot, filt,
    gated, grad_value, grad_gate, grad_filters,
    send1, recv1, send2, recv2, unpacked, result, xpad, gpad, toep, xcat, diag, gsend, grecv,
    ssem1, rsem1, ssem2, rsem2, gssem, grsem,
):
    seq = lax.axis_index("seq")
    ch = lax.axis_index("ch")

    barrier = pltpu.get_barrier_semaphore()

    def greet(k, carry):
        pl.semaphore_signal(barrier, inc=1, device_id=(partner(k, seq), ch), device_id_type=MESH)
        return carry

    lax.fori_loop(1, PEERS, greet, 0, unroll=7)
    for step in range(1, 4):
        pl.semaphore_signal(barrier, inc=1, device_id=(seq, (ch + step) & 3), device_id_type=MESH)

    flip = anti_identity(TOK, BF16)
    grad_conv = (cot[...].astype(F32) * gate[...].astype(F32)).astype(BF16)
    reverse = jnp.dot(grad_conv, flip, preferred_element_type=F32)
    both = jnp.concatenate(
        [value[...].astype(F32).reshape(PEERS, NFL, TOK), reverse.reshape(PEERS, NFL, TOK)], axis=1
    )
    send1[...] = both.astype(BF16)

    pl.semaphore_wait(barrier, PEERS + 2)

    def share1(k, carry):
        to = partner(k, seq)
        pltpu.make_async_remote_copy(
            src_ref=send1.at[to], dst_ref=recv1.at[seq], send_sem=ssem1, recv_sem=rsem1,
            device_id=(to, ch), device_id_type=MESH,
        ).start()
        return carry

    lax.fori_loop(1, PEERS, share1, 0, unroll=7)
    recv1[pl.ds(seq, 1)] = send1[pl.ds(seq, 1)]

    lane_zero = jnp.zeros((8, TOK), F32)
    for f in range(NFL):
        row = jnp.broadcast_to(filt[f : f + 1, 0:SPAN], (8, SPAN))
        row = jnp.concatenate([lane_zero, row], axis=1)
        for q in range(0, 16, 2):
            upper = pltpu.roll(row, 8 * q, 1, stride=1, stride_axis=0)
            lower = pltpu.roll(row, 8 * q + 8, 1, stride=1, stride_axis=0)
            toep[f, 8 * q : 8 * q + 16, :] = jnp.concatenate([upper, lower], axis=0).astype(BF16)
        toep[f, :, 0:TOK] = jnp.zeros((TOK, TOK), BF16)

    block = lax.broadcasted_iota(jnp.int32, (ROWS, TOK), 0)
    first = jnp.zeros((ROWS, TOK), jnp.int32)
    last = jnp.full((ROWS, TOK), ROWS, jnp.int32)
    edge = jnp.int32(0)
    for genome in range(4):
        first = jnp.where(block >= edge, edge, first)
        edge = edge + (lengths[genome] >> 8)
        last = jnp.minimum(last, jnp.where(block < edge, edge, ROWS))
    before = block - first
    after = last - 1 - block

    pltpu.make_async_copy(
        send1.at[pl.ds(0, PEERS - 1)], send1.at[pl.ds(0, PEERS - 1)], ssem1
    ).wait()
    pltpu.make_async_copy(
        recv1.at[pl.ds(0, PEERS - 1)], recv1.at[pl.ds(0, PEERS - 1)], rsem1
    ).wait()

    unpacked[...] = recv1[...].astype(F32).reshape(PEERS * 16, TOK)
    xpad[:, 0:LAGS, :] = jnp.zeros((NFL, LAGS, 256), F32)
    gpad[:, ROWS : ROWS + LAGS, :] = jnp.zeros((NFL, LAGS, 256), F32)
    flip2 = anti_identity(256, BF16)
    for f in range(NFL):
        xpad[f, LAGS : LAGS + ROWS, 0:TOK] = unpacked[pl.ds(f, ROWS, stride=32), :]
        xpad[f, LAGS : LAGS + ROWS, TOK:256] = unpacked[pl.ds(16 + f, ROWS, stride=32), :]
        gpad[f, 0:ROWS, TOK:256] = unpacked[pl.ds(8 + f, ROWS, stride=32), :]
        gpad[f, 0:ROWS, 0:TOK] = unpacked[pl.ds(24 + f, ROWS, stride=32), :]
        left, right = [], []
        for lag in range(LAGS):
            back = xpad[f, LAGS - lag : LAGS - lag + ROWS, :]
            ahead = gpad[f, lag : lag + ROWS, :]
            keep_x = jnp.concatenate([before >= lag] * 2, axis=1)
            keep_g = jnp.concatenate([after >= lag] * 2, axis=1)
            piece = jnp.concatenate(
                [jnp.where(keep_x, back, 0.0), jnp.where(keep_g, ahead, 0.0)], axis=0
            ).astype(BF16)
            xcat[f, :, 256 * lag : 256 * lag + 256] = piece[0:ROWS]
            left.append(piece)
            right.append(toep[f, :, 256 * lag + 128 : 256 * lag + 384])
            right.append(toep[f, :, 256 * lag : 256 * lag + 256])
        out = jnp.dot(
            jnp.concatenate(left, axis=1), jnp.concatenate(right, axis=0), preferred_element_type=F32
        )
        back = jnp.dot(out[ROWS:].astype(BF16), flip2, preferred_element_type=F32)
        result[pl.ds(f, ROWS, stride=32), :] = out[0:ROWS, 0:TOK]
        result[pl.ds(16 + f, ROWS, stride=32), :] = out[0:ROWS, TOK:256]
        result[pl.ds(8 + f, ROWS, stride=32), :] = back[:, 0:TOK]
        result[pl.ds(24 + f, ROWS, stride=32), :] = back[:, TOK:256]
    send2[...] = result[...].reshape(PEERS, 16, TOK).astype(BF16)

    def share2(k, carry):
        to = partner(k, seq)
        pltpu.make_async_remote_copy(
            src_ref=send2.at[to], dst_ref=recv2.at[seq], send_sem=ssem2, recv_sem=rsem2,
            device_id=(to, ch), device_id_type=MESH,
        ).start()
        return carry

    lax.fori_loop(1, PEERS, share2, 0, unroll=7)
    recv2[pl.ds(seq, 1)] = send2[pl.ds(seq, 1)]

    zero_tile = jnp.zeros((ROWS, TOK), BF16)
    for f in range(NFL):
        lhs = jnp.concatenate([gpad[f, 0:ROWS, TOK:256], gpad[f, 0:ROWS, 0:TOK]], axis=0).astype(BF16)
        tiles = []
        for d in range(2 * LAGS - 1, -1, -1):
            lag = d // 2
            if d % 2:
                if lag + 1 < LAGS:
                    even = xcat[f, :, 256 * lag + 384 : 256 * lag + 512]
                else:
                    even = zero_tile
                odd = xcat[f, :, 256 * lag : 256 * lag + 128]
            else:
                even = xcat[f, :, 256 * lag : 256 * lag + 128]
                odd = xcat[f, :, 256 * lag + 128 : 256 * lag + 256]
            tiles.append(jnp.concatenate([even, odd], axis=0))
        cross = lax.dot_general(
            lhs, jnp.concatenate(tiles, axis=1), (((0,), (0,)), ((), ())), preferred_element_type=F32
        )
        cross = jnp.concatenate([cross, jnp.zeros((TOK, TOK), F32)], axis=1)
        half = TOK // 2
        while half >= 8:
            cross = cross[0:half] + pltpu.roll(cross[half : 2 * half], half, 1)
            half //= 2
        cross = pltpu.roll(cross, 0, 1, stride=1, stride_axis=0)
        for tile in range(32):
            diag[8 * tile : 8 * tile + 8, :] = cross[:, TOK * tile : TOK * tile + TOK]
        total = diag[pl.ds(0, 32, stride=8), :]
        for j in range(1, 8):
            total = total + diag[pl.ds(j, 32, stride=8), :]
        total = jnp.dot(total, anti_identity(TOK, F32), precision=lax.Precision.HIGHEST, preferred_element_type=F32)
        gsend[0, 16 * f : 16 * f + 16, :] = total[16:32]
        gsend[1, 16 * f : 16 * f + 16, :] = total[0:16]

    for part in range(2):
        copy = pltpu.make_async_remote_copy(
            src_ref=gsend.at[part], dst_ref=grecv.at[ch], send_sem=gssem.at[part], recv_sem=grsem.at[ch],
            device_id=(seq, jnp.int32(part)), device_id_type=MESH,
        )
        pl.when(ch != part)(copy.start)

        @pl.when(ch == part)
        def _():
            grecv[pl.ds(ch, 1)] = gsend[part : part + 1]

    pltpu.make_async_copy(
        send2.at[pl.ds(0, PEERS - 1)], send2.at[pl.ds(0, PEERS - 1)], ssem2
    ).wait()
    pltpu.make_async_copy(
        recv2.at[pl.ds(0, PEERS - 1)], recv2.at[pl.ds(0, PEERS - 1)], rsem2
    ).wait()

    arrived = recv2[...].astype(F32)
    conv = arrived[:, 0:8].reshape(PEERS * NFL, TOK)
    gated[...] = (gate[...].astype(F32) * conv).astype(BF16)
    grad_gate[...] = (cot[...].astype(F32) * conv).astype(BF16)
    grad_value[...] = arrived[:, 8:16].reshape(PEERS * NFL, TOK).astype(BF16)

    for part in range(2):
        @pl.when(ch != part)
        def _():
            pltpu.make_async_copy(gsend.at[part], gsend.at[part], gssem.at[part]).wait()

    @pl.when(ch < 2)
    def _():
        for source in range(4):
            @pl.when(ch != source)
            def _():
                pltpu.make_async_copy(grecv.at[source], grecv.at[source], grsem.at[source]).wait()
        diag[0:128, :] = grecv[0] + grecv[1] + grecv[2] + grecv[3]
        for tile in range(16):
            grad_filters[:, TOK * (15 - tile) : TOK * (16 - tile)] = diag[pl.ds(tile, NFL, stride=16), :]

    @pl.when(ch >= 2)
    def _():
        grad_filters[...] = jnp.zeros((NFL, 2048), F32)


def per_device(value_in, gate_in, grad_out, filters, genome_lengths):
    shape = value_in.shape
    flat = (shape[1], shape[2])
    vmem = pl.BlockSpec(memory_space=pltpu.VMEM)
    messages = (PEERS, 16, TOK)
    outs = pl.pallas_call(
        kernel,
        out_shape=[jax.ShapeDtypeStruct(flat, BF16)] * 3 + [jax.ShapeDtypeStruct((NFL, 2048), F32)],
        in_specs=[
            pl.BlockSpec(memory_space=pltpu.SMEM), vmem, vmem, vmem,
            vmem,
        ],
        out_specs=[vmem] * 4,
        scratch_shapes=[
            pltpu.VMEM(messages, BF16), pltpu.VMEM(messages, BF16),
            pltpu.VMEM(messages, BF16), pltpu.VMEM(messages, BF16),
            pltpu.VMEM((PEERS * 16, TOK), F32), pltpu.VMEM((PEERS * 16, TOK), F32),
            pltpu.VMEM((NFL, ROWS + LAGS, 256), F32), pltpu.VMEM((NFL, ROWS + LAGS, 256), F32),
            pltpu.VMEM((NFL, TOK, SPAN + TOK), BF16),
            pltpu.VMEM((NFL, ROWS, SPAN), BF16),
            pltpu.VMEM((256, TOK), F32),
            pltpu.VMEM((2, 128, TOK), F32), pltpu.VMEM((4, 128, TOK), F32),
            pltpu.SemaphoreType.DMA, pltpu.SemaphoreType.DMA,
            pltpu.SemaphoreType.DMA, pltpu.SemaphoreType.DMA,
            pltpu.SemaphoreType.DMA((2,)), pltpu.SemaphoreType.DMA((4,)),
        ],
        compiler_params=pltpu.CompilerParams(
            collective_id=0, has_side_effects=True, vmem_limit_bytes=48 * 1024 * 1024
        ),
        name="hyena",
    )(genome_lengths, value_in.reshape(flat), gate_in.reshape(flat), grad_out.reshape(flat), filters)
    return (outs[0].reshape(shape), outs[1].reshape(shape), outs[2].reshape(shape), outs[3])


def solution(mesh):
    tokens = P("ch", None, "seq")
    return jax.shard_map(
        per_device,
        mesh=mesh,
        in_specs=(tokens, tokens, tokens, P("seq", None), P()),
        out_specs=(tokens, tokens, tokens, P("seq", "ch")),
        check_vma=False,
    )
```

```python
import functools

import jax
import jax.numpy as jnp
from jax import lax
from jax.experimental import pallas as pl
from jax.experimental.pallas import tpu as pltpu
from jax.sharding import PartitionSpec as P

MESH = pl.DeviceIdType.MESH
F32 = jnp.float32
BF16 = jnp.bfloat16

PEERS = 64
NFL = 8
TOK = 128
LAGS = 32
SPAN = LAGS * TOK
PARTS = 2
QUAD = NFL // PARTS


def anti_identity(n, dtype):
    row = lax.broadcasted_iota(jnp.int32, (n, n), 0)
    col = lax.broadcasted_iota(jnp.int32, (n, n), 1)
    return (row + col == n - 1).astype(dtype)


def partner(k, seq):
    z, y, c = seq >> 3, (seq >> 1) & 3, seq & 1
    dz, dy, dc = (3 * k) & 7, ((k >> 3) + k) & 3, k >> 5
    return (((((z + dz) & 7) << 2) + ((y + dy) & 3)) << 1) + (c ^ dc)


def kernel(
    lengths_hbm, value_hbm, gate_hbm, cot_hbm, filt_hbm,
    gated, grad_value, grad_gate, grad_filters,
    lengths, value, gate, cot, filt,
    send1, recv1, send2, recv2, unpacked, result, xpad, gpad, toep, xcat, diag, sums, gsend, grecv,
    insem, ssem1, rsem1, ssem2, rsem2, gssem, grsem,
):
    seq = lax.axis_index("seq")
    ch = lax.axis_index("ch")

    loads = [
        pltpu.make_async_copy(src, dst, insem.at[n])
        for n, (src, dst) in enumerate(
            [(cot_hbm, cot), (gate_hbm, gate), (value_hbm, value),
             (filt_hbm.at[:, pl.ds(0, SPAN)], filt), (lengths_hbm, lengths)]
        )
    ]
    for load in loads:
        load.start()

    barrier = pltpu.get_barrier_semaphore()

    def greet(k, carry):
        pl.semaphore_signal(barrier, inc=1, device_id=(partner(k, seq), ch), device_id_type=MESH)
        return carry

    lax.fori_loop(1, PEERS, greet, 0, unroll=7)
    for step in range(1, 4):
        pl.semaphore_signal(barrier, inc=1, device_id=(seq, (ch + step) & 3), device_id_type=MESH)

    upper = lax.broadcasted_iota(jnp.int32, (PEERS, NFL, TOK), 1) < QUAD
    flip = anti_identity(TOK, BF16)
    for load in loads[:3]:
        load.wait()
    grad_conv = (cot[...].astype(F32) * gate[...].astype(F32)).astype(BF16)
    reverse = jnp.dot(grad_conv, flip, preferred_element_type=F32).reshape(PEERS, NFL, TOK)
    wide = value[...].astype(F32).reshape(PEERS, NFL, TOK)
    send1[0] = jnp.where(upper, wide, pltpu.roll(reverse, QUAD, 1)).astype(BF16)
    send1[1] = jnp.where(upper, pltpu.roll(wide, QUAD, 1), reverse).astype(BF16)

    def exchange(src, dst, ssem, rsem, part):
        def share(k, carry):
            to = partner(k, seq)
            pltpu.make_async_remote_copy(
                src_ref=src.at[part, to], dst_ref=dst.at[part, seq],
                send_sem=ssem.at[part], recv_sem=rsem.at[part],
                device_id=(to, ch), device_id_type=MESH,
            ).start()
            return carry

        lax.fori_loop(1, PEERS, share, 0, unroll=7)
        dst[part, pl.ds(seq, 1)] = src[part, pl.ds(seq, 1)]

    def finish(buffer, sem, part):
        blocks = buffer.at[part, pl.ds(0, PEERS - 1)]
        pltpu.make_async_copy(blocks, blocks, sem.at[part]).wait()

    pl.semaphore_wait(barrier, PEERS + 2)
    for part in range(PARTS):
        exchange(send1, recv1, ssem1, rsem1, part)

    loads[3].wait()
    loads[4].wait()
    lane_zero = jnp.zeros((8, TOK), F32)
    for f in range(NFL):
        row = jnp.broadcast_to(filt[f : f + 1, :], (8, SPAN))
        row = jnp.concatenate([lane_zero, row], axis=1)
        for q in range(0, 16, 2):
            top = pltpu.roll(row, 8 * q, 1, stride=1, stride_axis=0)
            low = pltpu.roll(row, 8 * q + 8, 1, stride=1, stride_axis=0)
            toep[f, 8 * q : 8 * q + 16, :] = jnp.concatenate([top, low], axis=0).astype(BF16)

    block = lax.broadcasted_iota(jnp.int32, (PEERS, TOK), 0)
    first = jnp.zeros((PEERS, TOK), jnp.int32)
    last = jnp.full((PEERS, TOK), PEERS, jnp.int32)
    edge = jnp.int32(0)
    for genome in range(4):
        first = jnp.where(block >= edge, edge, first)
        edge = edge + (lengths[genome] >> 7)
        last = jnp.minimum(last, jnp.where(block < edge, edge, PEERS))
    before = block - first
    after = last - 1 - block

    xpad[:, 0:LAGS, :] = jnp.zeros((NFL, LAGS, TOK), F32)
    gpad[:, PEERS : PEERS + LAGS, :] = jnp.zeros((NFL, LAGS, TOK), F32)

    def convolve(part):
        unpacked[part] = recv1[part].astype(F32).reshape(PEERS * 8, TOK)
        for e in range(QUAD):
            f = QUAD * part + e
            xpad[f, LAGS : LAGS + PEERS, :] = unpacked[part, pl.ds(e, PEERS, stride=8), :]
            gpad[f, 0:PEERS, :] = unpacked[part, pl.ds(QUAD + e, PEERS, stride=8), :]
            left, right = [], []
            for lag in range(LAGS):
                back = jnp.where(before >= lag, xpad[f, LAGS - lag : LAGS - lag + PEERS, :], 0.0)
                ahead = jnp.where(after >= lag, gpad[f, lag : lag + PEERS, :], 0.0)
                piece = jnp.concatenate([back, ahead], axis=0).astype(BF16)
                xcat[f, :, TOK * lag : TOK * lag + TOK] = piece[0:PEERS]
                left.append(piece)
                right.append(toep[f, :, TOK * lag + TOK : TOK * lag + 2 * TOK])
            out = jnp.dot(
                jnp.concatenate(left, axis=1), jnp.concatenate(right, axis=0),
                preferred_element_type=F32,
            )
            back = jnp.dot(out[PEERS:].astype(BF16), flip, preferred_element_type=F32)
            result[part, pl.ds(e, PEERS, stride=8), :] = out[0:PEERS]
            result[part, pl.ds(QUAD + e, PEERS, stride=8), :] = back
        send2[part] = result[part].reshape(PEERS, 8, TOK).astype(BF16)

    def correlate(part):
        for e in range(QUAD):
            f = QUAD * part + e
            lhs = gpad[f, 0:PEERS, :].T.astype(BF16)
            rhs = [xcat[f, :, TOK * lag : TOK * lag + TOK] for lag in range(LAGS - 1, -1, -1)]
            cross = jnp.dot(lhs, jnp.concatenate(rhs, axis=1), preferred_element_type=F32)
            cross = jnp.concatenate([cross, jnp.zeros((TOK, TOK), F32)], axis=1)
            skew = pltpu.roll(cross[0:8], 0, 1, stride=1, stride_axis=0)
            for q in range(1, 16):
                skew = skew + pltpu.roll(cross[8 * q : 8 * q + 8], 8 * q, 1, stride=1, stride_axis=0)
            for tile in range(LAGS):
                diag[f, 8 * tile : 8 * tile + 8, :] = skew[:, TOK * tile : TOK * tile + TOK]
            total = diag[f, pl.ds(0, LAGS, stride=8), :]
            for j in range(1, 8):
                total = total + diag[f, pl.ds(j, LAGS, stride=8), :]
            sums[LAGS * f : LAGS * f + LAGS, :] = total

    for part in range(PARTS):
        finish(recv1, rsem1, part)
        convolve(part)
        exchange(send2, recv2, ssem2, rsem2, part)
    for part in range(PARTS):
        correlate(part)

    totals = jnp.dot(
        sums[...], anti_identity(TOK, F32), precision=lax.Precision.HIGHEST, preferred_element_type=F32
    )
    for f in range(NFL):
        gsend[0, 16 * f : 16 * f + 16, :] = totals[LAGS * f + 16 : LAGS * f + 32]
        gsend[1, 16 * f : 16 * f + 16, :] = totals[LAGS * f : LAGS * f + 16]

    for part in range(2):
        copy = pltpu.make_async_remote_copy(
            src_ref=gsend.at[part], dst_ref=grecv.at[ch], send_sem=gssem.at[part], recv_sem=grsem.at[ch],
            device_id=(seq, jnp.int32(part)), device_id_type=MESH,
        )
        pl.when(ch != part)(copy.start)

        @pl.when(ch == part)
        def _():
            grecv[pl.ds(ch, 1)] = gsend[part : part + 1]

    for part in range(PARTS):
        finish(recv2, rsem2, part)
    early = recv2[0].astype(F32)
    late = recv2[1].astype(F32)
    conv = jnp.where(upper, early, pltpu.roll(late, QUAD, 1)).reshape(PEERS * NFL, TOK)
    back = jnp.where(upper, pltpu.roll(early, QUAD, 1), late).reshape(PEERS * NFL, TOK)
    gated[...] = (gate[...].astype(F32) * conv).astype(BF16)
    grad_gate[...] = (cot[...].astype(F32) * conv).astype(BF16)
    grad_value[...] = back.astype(BF16)

    for part in range(PARTS):
        finish(send1, ssem1, part)
        finish(send2, ssem2, part)
    for part in range(2):
        @pl.when(ch != part)
        def _():
            pltpu.make_async_copy(gsend.at[part], gsend.at[part], gssem.at[part]).wait()

    @pl.when(ch < 2)
    def _():
        for source in range(4):
            @pl.when(ch != source)
            def _():
                pltpu.make_async_copy(grecv.at[source], grecv.at[source], grsem.at[source]).wait()
        sums[0:128, :] = grecv[0] + grecv[1] + grecv[2] + grecv[3]
        for tile in range(16):
            grad_filters[:, TOK * (15 - tile) : TOK * (16 - tile)] = sums[pl.ds(tile, NFL, stride=16), :]

    @pl.when(ch >= 2)
    def _():
        grad_filters[...] = jnp.zeros((NFL, 2048), F32)


def per_device(value_in, gate_in, grad_out, filters, genome_lengths):
    shape = value_in.shape
    flat = (shape[1], shape[2])
    vmem = pl.BlockSpec(memory_space=pltpu.VMEM)
    hbm = pl.BlockSpec(memory_space=pl.ANY)
    messages = pltpu.VMEM((PARTS, PEERS, 8, TOK), BF16)
    outs = pl.pallas_call(
        kernel,
        out_shape=[jax.ShapeDtypeStruct(flat, BF16)] * 3 + [jax.ShapeDtypeStruct((NFL, 2048), F32)],
        in_specs=[hbm] * 5,
        out_specs=[vmem] * 4,
        scratch_shapes=[
            pltpu.SMEM((4,), jnp.int32),
            pltpu.VMEM(flat, BF16), pltpu.VMEM(flat, BF16), pltpu.VMEM(flat, BF16),
            pltpu.VMEM((NFL, SPAN), F32),
            messages, messages, messages, messages,
            pltpu.VMEM((PARTS, PEERS * 8, TOK), F32), pltpu.VMEM((PARTS, PEERS * 8, TOK), F32),
            pltpu.VMEM((NFL, PEERS + LAGS, TOK), F32), pltpu.VMEM((NFL, PEERS + LAGS, TOK), F32),
            pltpu.VMEM((NFL, TOK, SPAN + TOK), BF16),
            pltpu.VMEM((NFL, PEERS, SPAN), BF16),
            pltpu.VMEM((NFL, 8 * LAGS, TOK), F32), pltpu.VMEM((NFL * LAGS, TOK), F32),
            pltpu.VMEM((2, 128, TOK), F32), pltpu.VMEM((4, 128, TOK), F32),
            pltpu.SemaphoreType.DMA((5,)),
            pltpu.SemaphoreType.DMA((PARTS,)), pltpu.SemaphoreType.DMA((PARTS,)),
            pltpu.SemaphoreType.DMA((PARTS,)), pltpu.SemaphoreType.DMA((PARTS,)),
            pltpu.SemaphoreType.DMA((2,)), pltpu.SemaphoreType.DMA((4,)),
        ],
        compiler_params=pltpu.CompilerParams(
            collective_id=0, has_side_effects=True, vmem_limit_bytes=58 * 1024 * 1024
        ),
        name="hyena",
    )(genome_lengths, value_in.reshape(flat), gate_in.reshape(flat), grad_out.reshape(flat), filters)
    return (outs[0].reshape(shape), outs[1].reshape(shape), outs[2].reshape(shape), outs[3])


def solution(mesh):
    tokens = P("ch", None, "seq")
    return jax.shard_map(
        per_device,
        mesh=mesh,
        in_specs=(tokens, tokens, tokens, P("seq", None), P()),
        out_specs=(tokens, tokens, tokens, P("seq", "ch")),
        check_vma=False,
    )
```

```python
import functools

import jax
import jax.numpy as jnp
from jax import lax
from jax.experimental import pallas as pl
from jax.experimental.pallas import tpu as pltpu
from jax.sharding import PartitionSpec as P

MESH = pl.DeviceIdType.MESH
F32 = jnp.float32
BF16 = jnp.bfloat16

PEERS = 64
NFL = 8
TOK = 128
LAGS = 32
SPAN = LAGS * TOK
PARTS = 2
QUAD = NFL // PARTS


def anti_identity(n, dtype):
    row = lax.broadcasted_iota(jnp.int32, (n, n), 0)
    col = lax.broadcasted_iota(jnp.int32, (n, n), 1)
    return (row + col == n - 1).astype(dtype)


def partner(k, seq):
    z, y, c = seq >> 3, (seq >> 1) & 3, seq & 1
    dz, dy, dc = (3 * k) & 7, ((k >> 3) + k) & 3, k >> 5
    return (((((z + dz) & 7) << 2) + ((y + dy) & 3)) << 1) + (c ^ dc)


def kernel(
    lengths_hbm, value_hbm, gate_hbm, cot_hbm, filt_hbm,
    recv2, gate, cot, grad_filters,
    lengths, value, filt,
    send1, recv1, send2, unpacked, result, xpad, gpad, toep, xcat, diag, sums, gsend, grecv,
    insem, ssem1, rsem1, ssem2, rsem2, gssem, grsem, ownsem,
):
    seq = lax.axis_index("seq")
    ch = lax.axis_index("ch")

    loads = [
        pltpu.make_async_copy(src, dst, insem.at[n])
        for n, (src, dst) in enumerate(
            [(cot_hbm, cot), (gate_hbm, gate), (value_hbm, value),
             (filt_hbm.at[:, pl.ds(0, SPAN)], filt), (lengths_hbm, lengths)]
        )
    ]
    for load in loads:
        load.start()

    barrier = pltpu.get_barrier_semaphore()

    def greet(k, carry):
        pl.semaphore_signal(barrier, inc=1, device_id=(partner(k, seq), ch), device_id_type=MESH)
        return carry

    lax.fori_loop(1, PEERS, greet, 0, unroll=7)
    for step in range(1, 4):
        pl.semaphore_signal(barrier, inc=1, device_id=(seq, (ch + step) & 3), device_id_type=MESH)

    upper = lax.broadcasted_iota(jnp.int32, (PEERS, NFL, TOK), 1) < QUAD
    flip = anti_identity(TOK, BF16)
    for load in loads[:3]:
        load.wait()
    grad_conv = (cot[...].astype(F32) * gate[...].astype(F32)).astype(BF16)
    reverse = jnp.dot(grad_conv, flip, preferred_element_type=F32).reshape(PEERS, NFL, TOK)
    wide = value[...].astype(F32).reshape(PEERS, NFL, TOK)
    send1[0] = jnp.where(upper, wide, pltpu.roll(reverse, QUAD, 1)).astype(BF16)
    send1[1] = jnp.where(upper, pltpu.roll(wide, QUAD, 1), reverse).astype(BF16)

    def exchange(src, dst, ssem, rsem, part):
        def share(k, carry):
            to = partner(k, seq)
            pltpu.make_async_remote_copy(
                src_ref=src.at[part, to], dst_ref=dst.at[part, seq],
                send_sem=ssem.at[part], recv_sem=rsem.at[part],
                device_id=(to, ch), device_id_type=MESH,
            ).start()
            return carry

        lax.fori_loop(1, PEERS, share, 0, unroll=7)
        own = pltpu.make_async_copy(src.at[part, seq], dst.at[part, seq], ownsem.at[part])
        own.start()
        return own

    def finish(buffer, sem, part):
        blocks = buffer.at[part, pl.ds(0, PEERS - 1)]
        pltpu.make_async_copy(blocks, blocks, sem.at[part]).wait()

    pl.semaphore_wait(barrier, PEERS + 2)
    own1 = [exchange(send1, recv1, ssem1, rsem1, part) for part in range(PARTS)]

    loads[3].wait()
    loads[4].wait()
    lane_zero = jnp.zeros((8, TOK), F32)
    for f in range(NFL):
        row = jnp.broadcast_to(filt[f : f + 1, :], (8, SPAN))
        row = jnp.concatenate([lane_zero, row], axis=1)
        for q in range(0, 16, 2):
            top = pltpu.roll(row, 8 * q, 1, stride=1, stride_axis=0)
            low = pltpu.roll(row, 8 * q + 8, 1, stride=1, stride_axis=0)
            toep[f, 8 * q : 8 * q + 16, :] = jnp.concatenate([top, low], axis=0).astype(BF16)

    block = lax.broadcasted_iota(jnp.int32, (PEERS, TOK), 0)
    first = jnp.zeros((PEERS, TOK), jnp.int32)
    last = jnp.full((PEERS, TOK), PEERS, jnp.int32)
    edge = jnp.int32(0)
    for genome in range(4):
        first = jnp.where(block >= edge, edge, first)
        edge = edge + (lengths[genome] >> 7)
        last = jnp.minimum(last, jnp.where(block < edge, edge, PEERS))
    before = block - first
    after = last - 1 - block

    xpad[:, 0:LAGS, :] = jnp.zeros((NFL, LAGS, TOK), F32)
    gpad[:, PEERS : PEERS + LAGS, :] = jnp.zeros((NFL, LAGS, TOK), F32)

    def convolve(part):
        unpacked[part] = recv1[part].astype(F32).reshape(PEERS * 8, TOK)
        for e in range(QUAD):
            f = QUAD * part + e
            xpad[f, LAGS : LAGS + PEERS, :] = unpacked[part, pl.ds(e, PEERS, stride=8), :]
            gpad[f, 0:PEERS, :] = unpacked[part, pl.ds(QUAD + e, PEERS, stride=8), :]
            left, right = [], []
            for lag in range(LAGS):
                back = jnp.where(before >= lag, xpad[f, LAGS - lag : LAGS - lag + PEERS, :], 0.0)
                ahead = jnp.where(after >= lag, gpad[f, lag : lag + PEERS, :], 0.0)
                piece = jnp.concatenate([back, ahead], axis=0).astype(BF16)
                xcat[f, :, TOK * lag : TOK * lag + TOK] = piece[0:PEERS]
                left.append(piece)
                right.append(toep[f, :, TOK * lag + TOK : TOK * lag + 2 * TOK])
            out = jnp.dot(
                jnp.concatenate(left, axis=1), jnp.concatenate(right, axis=0),
                preferred_element_type=F32,
            )
            back = jnp.dot(out[PEERS:].astype(BF16), flip, preferred_element_type=F32)
            result[part, pl.ds(e, PEERS, stride=8), :] = out[0:PEERS]
            result[part, pl.ds(QUAD + e, PEERS, stride=8), :] = back
        send2[part] = result[part].reshape(PEERS, 8, TOK).astype(BF16)

    def correlate(part):
        for e in range(QUAD):
            f = QUAD * part + e
            lhs = gpad[f, 0:PEERS, :].T.astype(BF16)
            rhs = [xcat[f, :, TOK * lag : TOK * lag + TOK] for lag in range(LAGS - 1, -1, -1)]
            cross = jnp.dot(lhs, jnp.concatenate(rhs, axis=1), preferred_element_type=F32)
            cross = jnp.concatenate([cross, jnp.zeros((TOK, TOK), F32)], axis=1)
            skew = pltpu.roll(cross[0:8], 0, 1, stride=1, stride_axis=0)
            for q in range(1, 16):
                skew = skew + pltpu.roll(cross[8 * q : 8 * q + 8], 8 * q, 1, stride=1, stride_axis=0)
            for tile in range(LAGS):
                diag[f, 8 * tile : 8 * tile + 8, :] = skew[:, TOK * tile : TOK * tile + TOK]
            total = diag[f, pl.ds(0, LAGS, stride=8), :]
            for j in range(1, 8):
                total = total + diag[f, pl.ds(j, LAGS, stride=8), :]
            sums[LAGS * f : LAGS * f + LAGS, :] = total

    def collect(half):
        totals = jnp.dot(
            sums[LAGS * QUAD * half : LAGS * QUAD * (half + 1), :], anti_identity(TOK, F32),
            precision=lax.Precision.HIGHEST, preferred_element_type=F32,
        )
        for e in range(QUAD):
            gsend[half, 0, 16 * e : 16 * e + 16, :] = totals[LAGS * e + 16 : LAGS * e + 32]
            gsend[half, 1, 16 * e : 16 * e + 16, :] = totals[LAGS * e : LAGS * e + 16]
        for to in range(2):
            copy = pltpu.make_async_remote_copy(
                src_ref=gsend.at[half, to], dst_ref=grecv.at[half, ch],
                send_sem=gssem.at[half, to], recv_sem=grsem.at[half, ch],
                device_id=(seq, jnp.int32(to)), device_id_type=MESH,
            )
            pl.when(ch != to)(copy.start)

            @pl.when(ch == to)
            def _():
                grecv[half, pl.ds(ch, 1)] = gsend[half, to : to + 1]

    own2 = []
    for part in range(PARTS):
        finish(recv1, rsem1, part)
        own1[part].wait()
        convolve(part)
        own2.append(exchange(send2, recv2, ssem2, rsem2, part))
        correlate(part)
        collect(part)

    @pl.when(ch < 2)
    def _():
        for half in range(PARTS):
            for source in range(4):
                @pl.when(ch != source)
                def _():
                    piece = grecv.at[half, source]
                    pltpu.make_async_copy(piece, piece, grsem.at[half, source]).wait()
            sums[64 * half : 64 * half + 64, :] = (
                grecv[half, 0] + grecv[half, 1] + grecv[half, 2] + grecv[half, 3]
            )
        for tile in range(16):
            grad_filters[:, TOK * (15 - tile) : TOK * (16 - tile)] = sums[pl.ds(tile, NFL, stride=16), :]

    @pl.when(ch >= 2)
    def _():
        grad_filters[...] = jnp.zeros((NFL, 2048), F32)

    for part in range(PARTS):
        finish(recv2, rsem2, part)
        own2[part].wait()
        finish(send1, ssem1, part)
        finish(send2, ssem2, part)
        for to in range(2):
            @pl.when(ch != to)
            def _():
                piece = gsend.at[part, to]
                pltpu.make_async_copy(piece, piece, gssem.at[part, to]).wait()


def gating(recv2, gate, cot, part_filters, gated, grad_value, grad_gate, grad_filters, out1, out2, out3, sem):
    filters = pltpu.make_async_copy(part_filters, grad_filters, sem.at[3])
    filters.start()
    upper = lax.broadcasted_iota(jnp.int32, (PEERS, NFL, TOK), 1) < QUAD
    early = recv2[0].astype(F32)
    late = recv2[1].astype(F32)
    back = jnp.where(upper, pltpu.roll(early, QUAD, 1), late).reshape(PEERS * NFL, TOK)
    out1[...] = back.astype(BF16)
    store1 = pltpu.make_async_copy(out1, grad_value, sem.at[0])
    store1.start()
    conv = jnp.where(upper, early, pltpu.roll(late, QUAD, 1)).reshape(PEERS * NFL, TOK)
    out2[...] = (gate[...].astype(F32) * conv).astype(BF16)
    store2 = pltpu.make_async_copy(out2, gated, sem.at[1])
    store2.start()
    out3[...] = (cot[...].astype(F32) * conv).astype(BF16)
    store3 = pltpu.make_async_copy(out3, grad_gate, sem.at[2])
    store3.start()
    for store in (filters, store1, store2, store3):
        store.wait()


def per_device(value_in, gate_in, grad_out, filters, genome_lengths):
    shape = value_in.shape
    flat = (shape[1], shape[2])
    hbm = pl.BlockSpec(memory_space=pltpu.HBM)
    messages = pltpu.VMEM((PARTS, PEERS, 8, TOK), BF16)
    flats = [array.reshape(flat) for array in (value_in, gate_in, grad_out)]
    tail = jax.ShapeDtypeStruct((NFL, 2048), F32)
    vmem = pl.BlockSpec(memory_space=pltpu.VMEM)
    held = [
        pltpu.with_memory_space_constraint(array, pltpu.HBM)
        for array in (genome_lengths, *flats, filters)
    ]
    outs = pl.pallas_call(
        kernel,
        out_shape=[
            jax.ShapeDtypeStruct((PARTS, PEERS, 8, TOK), BF16),
            jax.ShapeDtypeStruct(flat, BF16), jax.ShapeDtypeStruct(flat, BF16), tail,
        ],
        in_specs=[hbm] * 5,
        out_specs=[vmem] * 4,
        scratch_shapes=[
            pltpu.SMEM((4,), jnp.int32),
            pltpu.VMEM(flat, BF16),
            pltpu.VMEM((NFL, SPAN), F32),
            messages, messages, messages,
            pltpu.VMEM((PARTS, PEERS * 8, TOK), F32), pltpu.VMEM((PARTS, PEERS * 8, TOK), F32),
            pltpu.VMEM((NFL, PEERS + LAGS, TOK), F32), pltpu.VMEM((NFL, PEERS + LAGS, TOK), F32),
            pltpu.VMEM((NFL, TOK, SPAN + TOK), BF16),
            pltpu.VMEM((NFL, PEERS, SPAN), BF16),
            pltpu.VMEM((NFL, 8 * LAGS, TOK), F32), pltpu.VMEM((NFL * LAGS, TOK), F32),
            pltpu.VMEM((PARTS, 2, 64, TOK), F32), pltpu.VMEM((PARTS, 4, 64, TOK), F32),
            pltpu.SemaphoreType.DMA((5,)),
            pltpu.SemaphoreType.DMA((PARTS,)), pltpu.SemaphoreType.DMA((PARTS,)),
            pltpu.SemaphoreType.DMA((PARTS,)), pltpu.SemaphoreType.DMA((PARTS,)),
            pltpu.SemaphoreType.DMA((PARTS, 2)), pltpu.SemaphoreType.DMA((PARTS, 4)),
            pltpu.SemaphoreType.DMA((PARTS,)),
        ],
        compiler_params=pltpu.CompilerParams(
            collective_id=0, has_side_effects=True, vmem_limit_bytes=40 * 1024 * 1024
        ),
        name="hyena",
    )(*held)
    outs = pl.pallas_call(
        gating,
        out_shape=[jax.ShapeDtypeStruct(flat, BF16)] * 3 + [tail],
        in_specs=[vmem] * 4,
        out_specs=[hbm] * 4,
        scratch_shapes=[pltpu.VMEM(flat, BF16)] * 3 + [pltpu.SemaphoreType.DMA((4,))],
        compiler_params=pltpu.CompilerParams(vmem_limit_bytes=8 * 1024 * 1024),
        name="gating",
    )(*outs)
    return (outs[0].reshape(shape), outs[1].reshape(shape), outs[2].reshape(shape), outs[3])


def solution(mesh):
    tokens = P("ch", None, "seq")
    return jax.shard_map(
        per_device,
        mesh=mesh,
        in_specs=(tokens, tokens, tokens, P("seq", None), P()),
        out_specs=(tokens, tokens, tokens, P("seq", "ch")),
        check_vma=False,
    )
```

```python
import functools

import jax
import jax.numpy as jnp
from jax import lax
from jax.experimental import pallas as pl
from jax.experimental.pallas import tpu as pltpu
from jax.sharding import PartitionSpec as P

MESH = pl.DeviceIdType.MESH
F32 = jnp.float32
BF16 = jnp.bfloat16

PEERS = 64
NFL = 8
TOK = 128
LAGS = 32
SPAN = LAGS * TOK
PARTS = 2
QUAD = NFL // PARTS


def anti_identity(n, dtype):
    row = lax.broadcasted_iota(jnp.int32, (n, n), 0)
    col = lax.broadcasted_iota(jnp.int32, (n, n), 1)
    return (row + col == n - 1).astype(dtype)


def partner(k, seq):
    z, y, c = seq >> 3, (seq >> 1) & 3, seq & 1
    k = (PEERS - k) & (PEERS - 1)
    near = (k >> 3) + 1
    dz = ((near >> 1) * (1 - 2 * (near & 1))) & 7
    dy, dc = (k >> 1) & 3, k & 1
    return (((((z + dz) & 7) << 2) + ((y + dy) & 3)) << 1) + (c ^ dc)


def kernel(
    lengths_hbm, value_hbm, gate_hbm, cot_hbm, filt_hbm,
    recv2, gate, cot, grad_filters,
    lengths, value, filt,
    send1, recv1, send2, unpacked, result, xpad, gpad, toep, xcat, diag, sums, gsend, grecv,
    insem, ssem1, rsem1, ssem2, rsem2, gssem, grsem, ownsem,
):
    seq = lax.axis_index("seq")
    ch = lax.axis_index("ch")

    loads = [
        pltpu.make_async_copy(src, dst, insem.at[n])
        for n, (src, dst) in enumerate(
            [(cot_hbm, cot), (gate_hbm, gate), (value_hbm, value),
             (filt_hbm.at[:, pl.ds(0, SPAN)], filt), (lengths_hbm, lengths)]
        )
    ]
    for load in loads:
        load.start()

    barrier = pltpu.get_barrier_semaphore()

    def greet(k, carry):
        pl.semaphore_signal(barrier, inc=1, device_id=(partner(k, seq), ch), device_id_type=MESH)
        return carry

    lax.fori_loop(1, PEERS, greet, 0, unroll=7)
    for step in range(1, 4):
        pl.semaphore_signal(barrier, inc=1, device_id=(seq, (ch + step) & 3), device_id_type=MESH)

    upper = lax.broadcasted_iota(jnp.int32, (PEERS, NFL, TOK), 1) < QUAD
    flip = anti_identity(TOK, BF16)
    for load in loads[:3]:
        load.wait()
    grad_conv = (cot[...].astype(F32) * gate[...].astype(F32)).astype(BF16)
    reverse = jnp.dot(grad_conv, flip, preferred_element_type=F32).reshape(PEERS, NFL, TOK)
    wide = value[...].astype(F32).reshape(PEERS, NFL, TOK)
    send1[0] = jnp.where(upper, wide, pltpu.roll(reverse, QUAD, 1)).astype(BF16)
    send1[1] = jnp.where(upper, pltpu.roll(wide, QUAD, 1), reverse).astype(BF16)

    def exchange(src, dst, ssem, rsem, part):
        def share(k, carry):
            to = partner(k, seq)
            pltpu.make_async_remote_copy(
                src_ref=src.at[part, to], dst_ref=dst.at[part, seq],
                send_sem=ssem.at[part], recv_sem=rsem.at[part],
                device_id=(to, ch), device_id_type=MESH,
            ).start()
            return carry

        lax.fori_loop(1, PEERS, share, 0, unroll=7)
        own = pltpu.make_async_copy(src.at[part, seq], dst.at[part, seq], ownsem.at[part])
        own.start()
        return own

    def finish(buffer, sem, part):
        blocks = buffer.at[part, pl.ds(0, PEERS - 1)]
        pltpu.make_async_copy(blocks, blocks, sem.at[part]).wait()

    pl.semaphore_wait(barrier, PEERS + 2)
    own1 = [exchange(send1, recv1, ssem1, rsem1, part) for part in range(PARTS)]

    loads[3].wait()
    loads[4].wait()
    lane_zero = jnp.zeros((8, TOK), F32)
    for f in range(NFL):
        row = jnp.broadcast_to(filt[f : f + 1, :], (8, SPAN))
        row = jnp.concatenate([lane_zero, row], axis=1)
        for q in range(0, 16, 2):
            top = pltpu.roll(row, 8 * q, 1, stride=1, stride_axis=0)
            low = pltpu.roll(row, 8 * q + 8, 1, stride=1, stride_axis=0)
            toep[f, 8 * q : 8 * q + 16, :] = jnp.concatenate([top, low], axis=0).astype(BF16)

    block = lax.broadcasted_iota(jnp.int32, (PEERS, TOK), 0)
    first = jnp.zeros((PEERS, TOK), jnp.int32)
    last = jnp.full((PEERS, TOK), PEERS, jnp.int32)
    edge = jnp.int32(0)
    for genome in range(4):
        first = jnp.where(block >= edge, edge, first)
        edge = edge + (lengths[genome] >> 7)
        last = jnp.minimum(last, jnp.where(block < edge, edge, PEERS))
    before = block - first
    after = last - 1 - block

    xpad[:, 0:LAGS, :] = jnp.zeros((NFL, LAGS, TOK), F32)
    gpad[:, PEERS : PEERS + LAGS, :] = jnp.zeros((NFL, LAGS, TOK), F32)

    def convolve(part):
        unpacked[part] = recv1[part].astype(F32).reshape(PEERS * 8, TOK)
        backs = []
        for e in range(QUAD):
            f = QUAD * part + e
            xpad[f, LAGS : LAGS + PEERS, :] = unpacked[part, pl.ds(e, PEERS, stride=8), :]
            gpad[f, 0:PEERS, :] = unpacked[part, pl.ds(QUAD + e, PEERS, stride=8), :]
            left, right = [], []
            for lag in range(LAGS):
                back = jnp.where(before >= lag, xpad[f, LAGS - lag : LAGS - lag + PEERS, :], 0.0)
                ahead = jnp.where(after >= lag, gpad[f, lag : lag + PEERS, :], 0.0)
                piece = jnp.concatenate([back, ahead], axis=0).astype(BF16)
                xcat[f, :, TOK * lag : TOK * lag + TOK] = piece[0:PEERS]
                left.append(piece)
                right.append(toep[f, :, TOK * lag + TOK : TOK * lag + 2 * TOK])
            out = jnp.dot(
                jnp.concatenate(left, axis=1), jnp.concatenate(right, axis=0),
                preferred_element_type=F32,
            )
            result[part, pl.ds(e, PEERS, stride=8), :] = out[0:PEERS]
            backs.append(out[PEERS:].astype(BF16))
        back = jnp.dot(jnp.concatenate(backs, axis=0), flip, preferred_element_type=F32)
        for e in range(QUAD):
            result[part, pl.ds(QUAD + e, PEERS, stride=8), :] = back[PEERS * e : PEERS * e + PEERS]
        send2[part] = result[part].reshape(PEERS, 8, TOK).astype(BF16)

    def correlate(part):
        for e in range(QUAD):
            f = QUAD * part + e
            lhs = gpad[f, 0:PEERS, :].T.astype(BF16)
            rhs = [xcat[f, :, TOK * lag : TOK * lag + TOK] for lag in range(LAGS - 1, -1, -1)]
            cross = jnp.dot(lhs, jnp.concatenate(rhs, axis=1), preferred_element_type=F32)
            cross = jnp.concatenate([cross, jnp.zeros((TOK, TOK), F32)], axis=1)
            skew = pltpu.roll(cross[0:8], 0, 1, stride=1, stride_axis=0)
            for q in range(1, 16):
                skew = skew + pltpu.roll(cross[8 * q : 8 * q + 8], 8 * q, 1, stride=1, stride_axis=0)
            for tile in range(LAGS):
                diag[f, 8 * tile : 8 * tile + 8, :] = skew[:, TOK * tile : TOK * tile + TOK]
            total = diag[f, pl.ds(0, LAGS, stride=8), :]
            for j in range(1, 8):
                total = total + diag[f, pl.ds(j, LAGS, stride=8), :]
            sums[LAGS * f : LAGS * f + LAGS, :] = total

    def collect(half):
        for e in range(QUAD):
            f = QUAD * half + e
            gsend[half, 0, 16 * e : 16 * e + 16, :] = sums[LAGS * f + 16 : LAGS * f + 32]
            gsend[half, 1, 16 * e : 16 * e + 16, :] = sums[LAGS * f : LAGS * f + 16]
        for to in range(2):
            copy = pltpu.make_async_remote_copy(
                src_ref=gsend.at[half, to], dst_ref=grecv.at[half, ch],
                send_sem=gssem.at[half, to], recv_sem=grsem.at[half, ch],
                device_id=(seq, jnp.int32(to)), device_id_type=MESH,
            )
            pl.when(ch != to)(copy.start)

            @pl.when(ch == to)
            def _():
                grecv[half, pl.ds(ch, 1)] = gsend[half, to : to + 1]

    own2 = []
    for part in range(PARTS):
        finish(recv1, rsem1, part)
        own1[part].wait()
        convolve(part)
        own2.append(exchange(send2, recv2, ssem2, rsem2, part))
        correlate(part)
        collect(part)

    @pl.when(ch < 2)
    def _():
        for half in range(PARTS):
            for source in range(4):
                @pl.when(ch != source)
                def _():
                    piece = grecv.at[half, source]
                    pltpu.make_async_copy(piece, piece, grsem.at[half, source]).wait()
            sums[64 * half : 64 * half + 64, :] = jnp.dot(
                grecv[half, 0] + grecv[half, 1] + grecv[half, 2] + grecv[half, 3],
                anti_identity(TOK, F32),
                precision=lax.Precision.HIGHEST, preferred_element_type=F32,
            )
        for tile in range(16):
            grad_filters[:, TOK * (15 - tile) : TOK * (16 - tile)] = sums[pl.ds(tile, NFL, stride=16), :]

    @pl.when(ch >= 2)
    def _():
        grad_filters[...] = jnp.zeros((NFL, 2048), F32)

    for part in range(PARTS):
        finish(recv2, rsem2, part)
        own2[part].wait()
        finish(send1, ssem1, part)
        finish(send2, ssem2, part)
        for to in range(2):
            @pl.when(ch != to)
            def _():
                piece = gsend.at[part, to]
                pltpu.make_async_copy(piece, piece, gssem.at[part, to]).wait()


def gating(recv2, gate, cot, part_filters, gated, grad_value, grad_gate, grad_filters, out1, out2, out3, sem):
    filters = pltpu.make_async_copy(part_filters, grad_filters, sem.at[3])
    filters.start()
    upper = lax.broadcasted_iota(jnp.int32, (PEERS, NFL, TOK), 1) < QUAD
    early = recv2[0].astype(F32)
    late = recv2[1].astype(F32)
    back = jnp.where(upper, pltpu.roll(early, QUAD, 1), late).reshape(PEERS * NFL, TOK)
    out1[...] = back.astype(BF16)
    store1 = pltpu.make_async_copy(out1, grad_value, sem.at[0])
    store1.start()
    conv = jnp.where(upper, early, pltpu.roll(late, QUAD, 1)).reshape(PEERS * NFL, TOK)
    out2[...] = (gate[...].astype(F32) * conv).astype(BF16)
    store2 = pltpu.make_async_copy(out2, gated, sem.at[1])
    store2.start()
    out3[...] = (cot[...].astype(F32) * conv).astype(BF16)
    store3 = pltpu.make_async_copy(out3, grad_gate, sem.at[2])
    store3.start()
    for store in (filters, store1, store2, store3):
        store.wait()


def per_device(value_in, gate_in, grad_out, filters, genome_lengths):
    shape = value_in.shape
    flat = (shape[1], shape[2])
    hbm = pl.BlockSpec(memory_space=pltpu.HBM)
    messages = pltpu.VMEM((PARTS, PEERS, 8, TOK), BF16)
    flats = [array.reshape(flat) for array in (value_in, gate_in, grad_out)]
    tail = jax.ShapeDtypeStruct((NFL, 2048), F32)
    vmem = pl.BlockSpec(memory_space=pltpu.VMEM)
    held = [
        pltpu.with_memory_space_constraint(array, pltpu.HBM)
        for array in (genome_lengths, *flats, filters)
    ]
    outs = pl.pallas_call(
        kernel,
        out_shape=[
            jax.ShapeDtypeStruct((PARTS, PEERS, 8, TOK), BF16),
            jax.ShapeDtypeStruct(flat, BF16), jax.ShapeDtypeStruct(flat, BF16), tail,
        ],
        in_specs=[hbm] * 5,
        out_specs=[vmem] * 4,
        scratch_shapes=[
            pltpu.SMEM((4,), jnp.int32),
            pltpu.VMEM(flat, BF16),
            pltpu.VMEM((NFL, SPAN), F32),
            messages, messages, messages,
            pltpu.VMEM((PARTS, PEERS * 8, TOK), F32), pltpu.VMEM((PARTS, PEERS * 8, TOK), F32),
            pltpu.VMEM((NFL, PEERS + LAGS, TOK), F32), pltpu.VMEM((NFL, PEERS + LAGS, TOK), F32),
            pltpu.VMEM((NFL, TOK, SPAN + TOK), BF16),
            pltpu.VMEM((NFL, PEERS, SPAN), BF16),
            pltpu.VMEM((NFL, 8 * LAGS, TOK), F32), pltpu.VMEM((NFL * LAGS, TOK), F32),
            pltpu.VMEM((PARTS, 2, 64, TOK), F32), pltpu.VMEM((PARTS, 4, 64, TOK), F32),
            pltpu.SemaphoreType.DMA((5,)),
            pltpu.SemaphoreType.DMA((PARTS,)), pltpu.SemaphoreType.DMA((PARTS,)),
            pltpu.SemaphoreType.DMA((PARTS,)), pltpu.SemaphoreType.DMA((PARTS,)),
            pltpu.SemaphoreType.DMA((PARTS, 2)), pltpu.SemaphoreType.DMA((PARTS, 4)),
            pltpu.SemaphoreType.DMA((PARTS,)),
        ],
        compiler_params=pltpu.CompilerParams(
            collective_id=0, has_side_effects=True, vmem_limit_bytes=40 * 1024 * 1024
        ),
        name="hyena",
    )(*held)
    outs = pl.pallas_call(
        gating,
        out_shape=[jax.ShapeDtypeStruct(flat, BF16)] * 3 + [tail],
        in_specs=[vmem] * 4,
        out_specs=[hbm] * 4,
        scratch_shapes=[pltpu.VMEM(flat, BF16)] * 3 + [pltpu.SemaphoreType.DMA((4,))],
        compiler_params=pltpu.CompilerParams(vmem_limit_bytes=8 * 1024 * 1024),
        name="gating",
    )(*outs)
    return (outs[0].reshape(shape), outs[1].reshape(shape), outs[2].reshape(shape), outs[3])


def solution(mesh):
    tokens = P("ch", None, "seq")
    return jax.shard_map(
        per_device,
        mesh=mesh,
        in_specs=(tokens, tokens, tokens, P("seq", None), P()),
        out_specs=(tokens, tokens, tokens, P("seq", "ch")),
        check_vma=False,
    )
```

```python
import functools

import jax
import jax.numpy as jnp
from jax import lax
from jax.experimental import pallas as pl
from jax.experimental.pallas import tpu as pltpu
from jax.sharding import PartitionSpec as P

MESH = pl.DeviceIdType.MESH
F32 = jnp.float32
BF16 = jnp.bfloat16

PEERS = 64
NFL = 8
TOK = 128
LAGS = 32
SPAN = LAGS * TOK
PARTS = 2
QUAD = NFL // PARTS


def anti_identity(n, dtype):
    row = lax.broadcasted_iota(jnp.int32, (n, n), 0)
    col = lax.broadcasted_iota(jnp.int32, (n, n), 1)
    return (row + col == n - 1).astype(dtype)


def partner(k, seq):
    z, y, c = seq >> 3, (seq >> 1) & 3, seq & 1
    k = (PEERS - k) & (PEERS - 1)
    near = (k >> 3) + 1
    dz = ((near >> 1) * (1 - 2 * (near & 1))) & 7
    dy, dc = (k >> 1) & 3, k & 1
    return (((((z + dz) & 7) << 2) + ((y + dy) & 3)) << 1) + (c ^ dc)


def kernel(
    lengths_hbm, value_hbm, gate_hbm, cot_hbm, filt_hbm,
    recv2, gate, cot, grad_filters,
    lengths, value, filt,
    send1, recv1, send2, unpacked, result, xpad, gpad, toep, xcat, diag, sums, gsend, grecv,
    insem, ssem1, rsem1, ssem2, rsem2, gssem, grsem, ownsem,
):
    seq = lax.axis_index("seq")
    ch = lax.axis_index("ch")

    loads = [
        pltpu.make_async_copy(src, dst, insem.at[n])
        for n, (src, dst) in enumerate(
            [(cot_hbm, cot), (gate_hbm, gate), (value_hbm, value),
             (filt_hbm.at[:, pl.ds(0, SPAN)], filt), (lengths_hbm, lengths)]
        )
    ]
    for load in loads:
        load.start()

    barrier = pltpu.get_barrier_semaphore()

    def greet(k, carry):
        pl.semaphore_signal(barrier, inc=1, device_id=(partner(k, seq), ch), device_id_type=MESH)
        return carry

    lax.fori_loop(1, PEERS, greet, 0, unroll=7)
    for step in range(1, 4):
        pl.semaphore_signal(barrier, inc=1, device_id=(seq, (ch + step) & 3), device_id_type=MESH)

    upper = lax.broadcasted_iota(jnp.int32, (PEERS, NFL, TOK), 1) < QUAD
    flip = anti_identity(TOK, BF16)
    for load in loads[:3]:
        load.wait()
    grad_conv = (cot[...].astype(F32) * gate[...].astype(F32)).astype(BF16)
    reverse = jnp.dot(grad_conv, flip, preferred_element_type=F32).reshape(PEERS, NFL, TOK)
    wide = value[...].astype(F32).reshape(PEERS, NFL, TOK)
    send1[0] = jnp.where(upper, wide, pltpu.roll(reverse, QUAD, 1)).astype(BF16)
    send1[1] = jnp.where(upper, pltpu.roll(wide, QUAD, 1), reverse).astype(BF16)

    def exchange(src, dst, ssem, rsem, part):
        def share(k, carry):
            to = partner(k, seq)
            pltpu.make_async_remote_copy(
                src_ref=src.at[part, to], dst_ref=dst.at[part, seq],
                send_sem=ssem.at[part], recv_sem=rsem.at[part],
                device_id=(to, ch), device_id_type=MESH,
            ).start()
            return carry

        lax.fori_loop(1, PEERS, share, 0, unroll=7)
        own = pltpu.make_async_copy(src.at[part, seq], dst.at[part, seq], ownsem.at[part])
        own.start()
        return own

    def finish(buffer, sem, part):
        blocks = buffer.at[part, pl.ds(0, PEERS - 1)]
        pltpu.make_async_copy(blocks, blocks, sem.at[part]).wait()

    pl.semaphore_wait(barrier, PEERS + 2)
    own1 = [exchange(send1, recv1, ssem1, rsem1, part) for part in range(PARTS)]

    loads[3].wait()
    loads[4].wait()
    lane_zero = jnp.zeros((8, TOK), F32)
    for f in range(NFL):
        row = jnp.broadcast_to(filt[f : f + 1, :], (8, SPAN))
        row = jnp.concatenate([lane_zero, row], axis=1)
        for q in range(0, 16, 2):
            top = pltpu.roll(row, 8 * q, 1, stride=1, stride_axis=0)
            low = pltpu.roll(row, 8 * q + 8, 1, stride=1, stride_axis=0)
            toep[f, 8 * q : 8 * q + 16, :] = jnp.concatenate([top, low], axis=0).astype(BF16)

    block = lax.broadcasted_iota(jnp.int32, (PEERS, TOK), 0)
    first = jnp.zeros((PEERS, TOK), jnp.int32)
    last = jnp.full((PEERS, TOK), PEERS, jnp.int32)
    edge = jnp.int32(0)
    for genome in range(4):
        first = jnp.where(block >= edge, edge, first)
        edge = edge + (lengths[genome] >> 7)
        last = jnp.minimum(last, jnp.where(block < edge, edge, PEERS))
    before = block - first
    after = last - 1 - block

    xpad[:, 0:LAGS, :] = jnp.zeros((NFL, LAGS, TOK), F32)
    gpad[:, PEERS : PEERS + LAGS, :] = jnp.zeros((NFL, LAGS, TOK), F32)

    def convolve(part):
        unpacked[part] = recv1[part].astype(F32).reshape(PEERS * 8, TOK)
        backs = []
        for e in range(QUAD):
            f = QUAD * part + e
            xpad[f, LAGS : LAGS + PEERS, :] = unpacked[part, pl.ds(e, PEERS, stride=8), :]
            gpad[f, 0:PEERS, :] = unpacked[part, pl.ds(QUAD + e, PEERS, stride=8), :]
            left, right = [], []
            for lag in range(LAGS):
                back = jnp.where(before >= lag, xpad[f, LAGS - lag : LAGS - lag + PEERS, :], 0.0)
                ahead = jnp.where(after >= lag, gpad[f, lag : lag + PEERS, :], 0.0)
                piece = jnp.concatenate([back, ahead], axis=0).astype(BF16)
                xcat[f, :, TOK * lag : TOK * lag + TOK] = piece[0:PEERS]
                left.append(piece)
                right.append(toep[f, :, TOK * lag + TOK : TOK * lag + 2 * TOK])
            out = jnp.dot(
                jnp.concatenate(left, axis=1), jnp.concatenate(right, axis=0),
                preferred_element_type=F32,
            )
            result[part, pl.ds(e, PEERS, stride=8), :] = out[0:PEERS]
            backs.append(out[PEERS:].astype(BF16))
        back = jnp.dot(jnp.concatenate(backs, axis=0), flip, preferred_element_type=F32)
        for e in range(QUAD):
            result[part, pl.ds(QUAD + e, PEERS, stride=8), :] = back[PEERS * e : PEERS * e + PEERS]
        send2[part] = result[part].reshape(PEERS, 8, TOK).astype(BF16)

    def correlate(part):
        for e in range(QUAD):
            f = QUAD * part + e
            lhs = gpad[f, 0:PEERS, :].T.astype(BF16)
            rhs = [xcat[f, :, TOK * lag : TOK * lag + TOK] for lag in range(LAGS - 1, -1, -1)]
            cross = jnp.dot(lhs, jnp.concatenate(rhs, axis=1), preferred_element_type=F32)
            cross = jnp.concatenate([cross, jnp.zeros((TOK, TOK), F32)], axis=1)
            skew = pltpu.roll(cross[0:8], 0, 1, stride=1, stride_axis=0)
            for q in range(1, 16):
                skew = skew + pltpu.roll(cross[8 * q : 8 * q + 8], 8 * q, 1, stride=1, stride_axis=0)
            for tile in range(LAGS):
                diag[f, 8 * tile : 8 * tile + 8, :] = skew[:, TOK * tile : TOK * tile + TOK]
            total = diag[f, pl.ds(0, LAGS, stride=8), :]
            for j in range(1, 8):
                total = total + diag[f, pl.ds(j, LAGS, stride=8), :]
            sums[LAGS * f : LAGS * f + LAGS, :] = total

    def collect(half):
        for e in range(QUAD):
            f = QUAD * half + e
            gsend[half, 0, 16 * e : 16 * e + 16, :] = sums[LAGS * f + 16 : LAGS * f + 32]
            gsend[half, 1, 16 * e : 16 * e + 16, :] = sums[LAGS * f : LAGS * f + 16]
        for to in range(2):
            copy = pltpu.make_async_remote_copy(
                src_ref=gsend.at[half, to], dst_ref=grecv.at[half, ch],
                send_sem=gssem.at[half, to], recv_sem=grsem.at[half, ch],
                device_id=(seq, jnp.int32(to)), device_id_type=MESH,
            )
            pl.when(ch != to)(copy.start)

            @pl.when(ch == to)
            def _():
                grecv[half, pl.ds(ch, 1)] = gsend[half, to : to + 1]

    own2 = []
    for part in range(PARTS):
        finish(recv1, rsem1, part)
        own1[part].wait()
        convolve(part)
        own2.append(exchange(send2, recv2, ssem2, rsem2, part))
    for part in range(PARTS):
        correlate(part)
        collect(part)

    @pl.when(ch < 2)
    def _():
        for half in range(PARTS):
            for source in range(4):
                @pl.when(ch != source)
                def _():
                    piece = grecv.at[half, source]
                    pltpu.make_async_copy(piece, piece, grsem.at[half, source]).wait()
            sums[64 * half : 64 * half + 64, :] = jnp.dot(
                grecv[half, 0] + grecv[half, 1] + grecv[half, 2] + grecv[half, 3],
                anti_identity(TOK, F32),
                precision=lax.Precision.HIGHEST, preferred_element_type=F32,
            )
        for tile in range(16):
            grad_filters[:, TOK * (15 - tile) : TOK * (16 - tile)] = sums[pl.ds(tile, NFL, stride=16), :]

    @pl.when(ch >= 2)
    def _():
        grad_filters[...] = jnp.zeros((NFL, 2048), F32)

    for part in range(PARTS):
        finish(recv2, rsem2, part)
        own2[part].wait()
        finish(send1, ssem1, part)
        finish(send2, ssem2, part)
        for to in range(2):
            @pl.when(ch != to)
            def _():
                piece = gsend.at[part, to]
                pltpu.make_async_copy(piece, piece, gssem.at[part, to]).wait()


def gating(recv2, gate, cot, part_filters, gated, grad_value, grad_gate, grad_filters, out1, out2, out3, sem):
    filters = pltpu.make_async_copy(part_filters, grad_filters, sem.at[3])
    filters.start()
    upper = lax.broadcasted_iota(jnp.int32, (PEERS, NFL, TOK), 1) < QUAD
    early = recv2[0].astype(F32)
    late = recv2[1].astype(F32)
    back = jnp.where(upper, pltpu.roll(early, QUAD, 1), late).reshape(PEERS * NFL, TOK)
    out1[...] = back.astype(BF16)
    store1 = pltpu.make_async_copy(out1, grad_value, sem.at[0])
    store1.start()
    conv = jnp.where(upper, early, pltpu.roll(late, QUAD, 1)).reshape(PEERS * NFL, TOK)
    out2[...] = (gate[...].astype(F32) * conv).astype(BF16)
    store2 = pltpu.make_async_copy(out2, gated, sem.at[1])
    store2.start()
    out3[...] = (cot[...].astype(F32) * conv).astype(BF16)
    store3 = pltpu.make_async_copy(out3, grad_gate, sem.at[2])
    store3.start()
    for store in (filters, store1, store2, store3):
        store.wait()


def per_device(value_in, gate_in, grad_out, filters, genome_lengths):
    shape = value_in.shape
    flat = (shape[1], shape[2])
    hbm = pl.BlockSpec(memory_space=pltpu.HBM)
    messages = pltpu.VMEM((PARTS, PEERS, 8, TOK), BF16)
    flats = [array.reshape(flat) for array in (value_in, gate_in, grad_out)]
    tail = jax.ShapeDtypeStruct((NFL, 2048), F32)
    vmem = pl.BlockSpec(memory_space=pltpu.VMEM)
    held = [
        pltpu.with_memory_space_constraint(array, pltpu.HBM)
        for array in (genome_lengths, *flats, filters)
    ]
    outs = pl.pallas_call(
        kernel,
        out_shape=[
            jax.ShapeDtypeStruct((PARTS, PEERS, 8, TOK), BF16),
            jax.ShapeDtypeStruct(flat, BF16), jax.ShapeDtypeStruct(flat, BF16), tail,
        ],
        in_specs=[hbm] * 5,
        out_specs=[vmem] * 4,
        scratch_shapes=[
            pltpu.SMEM((4,), jnp.int32),
            pltpu.VMEM(flat, BF16),
            pltpu.VMEM((NFL, SPAN), F32),
            messages, messages, messages,
            pltpu.VMEM((PARTS, PEERS * 8, TOK), F32), pltpu.VMEM((PARTS, PEERS * 8, TOK), F32),
            pltpu.VMEM((NFL, PEERS + LAGS, TOK), F32), pltpu.VMEM((NFL, PEERS + LAGS, TOK), F32),
            pltpu.VMEM((NFL, TOK, SPAN + TOK), BF16),
            pltpu.VMEM((NFL, PEERS, SPAN), BF16),
            pltpu.VMEM((NFL, 8 * LAGS, TOK), F32), pltpu.VMEM((NFL * LAGS, TOK), F32),
            pltpu.VMEM((PARTS, 2, 64, TOK), F32), pltpu.VMEM((PARTS, 4, 64, TOK), F32),
            pltpu.SemaphoreType.DMA((5,)),
            pltpu.SemaphoreType.DMA((PARTS,)), pltpu.SemaphoreType.DMA((PARTS,)),
            pltpu.SemaphoreType.DMA((PARTS,)), pltpu.SemaphoreType.DMA((PARTS,)),
            pltpu.SemaphoreType.DMA((PARTS, 2)), pltpu.SemaphoreType.DMA((PARTS, 4)),
            pltpu.SemaphoreType.DMA((PARTS,)),
        ],
        compiler_params=pltpu.CompilerParams(
            collective_id=0, has_side_effects=True, vmem_limit_bytes=40 * 1024 * 1024
        ),
        name="hyena",
    )(*held)
    outs = pl.pallas_call(
        gating,
        out_shape=[jax.ShapeDtypeStruct(flat, BF16)] * 3 + [tail],
        in_specs=[vmem] * 4,
        out_specs=[hbm] * 4,
        scratch_shapes=[pltpu.VMEM(flat, BF16)] * 3 + [pltpu.SemaphoreType.DMA((4,))],
        compiler_params=pltpu.CompilerParams(vmem_limit_bytes=8 * 1024 * 1024),
        name="gating",
    )(*outs)
    return (outs[0].reshape(shape), outs[1].reshape(shape), outs[2].reshape(shape), outs[3])


def solution(mesh):
    tokens = P("ch", None, "seq")
    return jax.shard_map(
        per_device,
        mesh=mesh,
        in_specs=(tokens, tokens, tokens, P("seq", None), P()),
        out_specs=(tokens, tokens, tokens, P("seq", "ch")),
        check_vma=False,
    )
```

```python
import functools

import jax
import jax.numpy as jnp
from jax import lax
from jax.experimental import pallas as pl
from jax.experimental.pallas import tpu as pltpu
from jax.sharding import PartitionSpec as P

MESH = pl.DeviceIdType.MESH
F32 = jnp.float32
BF16 = jnp.bfloat16

PEERS = 64
NFL = 8
TOK = 128
LAGS = 32
SPAN = LAGS * TOK
PARTS = 2
QUAD = NFL // PARTS


def anti_identity(n, dtype):
    row = lax.broadcasted_iota(jnp.int32, (n, n), 0)
    col = lax.broadcasted_iota(jnp.int32, (n, n), 1)
    return (row + col == n - 1).astype(dtype)


def partner(k, seq):
    z, y, c = seq >> 3, (seq >> 1) & 3, seq & 1
    k = (PEERS - k) & (PEERS - 1)
    near = (k >> 3) + 1
    dz = ((near >> 1) * (1 - 2 * (near & 1))) & 7
    dy, dc = (k >> 1) & 3, k & 1
    return (((((z + dz) & 7) << 2) + ((y + dy) & 3)) << 1) + (c ^ dc)


def kernel(
    lengths_hbm, value_hbm, gate_hbm, cot_hbm, filt_hbm,
    recv2, gate, cot, grad_filters,
    lengths, value, filt,
    send1, recv1, send2, unpacked, result, xpad, gpad, toep, xcat, diag, sums, gsend, grecv,
    insem, ssem1, rsem1, ssem2, rsem2, gssem, grsem, ownsem,
):
    seq = lax.axis_index("seq")
    ch = lax.axis_index("ch")

    loads = [
        pltpu.make_async_copy(src, dst, insem.at[n])
        for n, (src, dst) in enumerate(
            [(cot_hbm, cot), (gate_hbm, gate), (value_hbm, value),
             (filt_hbm.at[:, pl.ds(0, SPAN)], filt), (lengths_hbm, lengths)]
        )
    ]
    for load in loads:
        load.start()

    barrier = pltpu.get_barrier_semaphore()

    def greet(k, carry):
        pl.semaphore_signal(barrier, inc=1, device_id=(partner(k, seq), ch), device_id_type=MESH)
        return carry

    lax.fori_loop(1, PEERS, greet, 0, unroll=7)
    for step in range(1, 4):
        pl.semaphore_signal(barrier, inc=1, device_id=(seq, (ch + step) & 3), device_id_type=MESH)

    upper = lax.broadcasted_iota(jnp.int32, (PEERS, NFL, TOK), 1) < QUAD
    flip = anti_identity(TOK, BF16)
    for load in loads[:3]:
        load.wait()
    grad_conv = (cot[...].astype(F32) * gate[...].astype(F32)).astype(BF16)
    reverse = jnp.dot(grad_conv, flip, preferred_element_type=F32).reshape(PEERS, NFL, TOK)
    wide = value[...].astype(F32).reshape(PEERS, NFL, TOK)
    send1[0] = jnp.where(upper, wide, pltpu.roll(reverse, QUAD, 1)).astype(BF16)
    send1[1] = jnp.where(upper, pltpu.roll(wide, QUAD, 1), reverse).astype(BF16)

    def exchange(src, dst, ssem, rsem, part):
        def share(k, carry):
            to = partner(k, seq)
            pltpu.make_async_remote_copy(
                src_ref=src.at[part, to], dst_ref=dst.at[part, seq],
                send_sem=ssem.at[part], recv_sem=rsem.at[part],
                device_id=(to, ch), device_id_type=MESH,
            ).start()
            return carry

        lax.fori_loop(1, PEERS, share, 0, unroll=7)
        own = pltpu.make_async_copy(src.at[part, seq], dst.at[part, seq], ownsem.at[part])
        own.start()
        return own

    def finish(buffer, sem, part):
        blocks = buffer.at[part, pl.ds(0, PEERS - 1)]
        pltpu.make_async_copy(blocks, blocks, sem.at[part]).wait()

    pl.semaphore_wait(barrier, PEERS + 2)
    own1 = [exchange(send1, recv1, ssem1, rsem1, part) for part in range(PARTS)]

    loads[3].wait()
    loads[4].wait()
    lane_zero = jnp.zeros((8, TOK), F32)
    for f in range(NFL):
        row = jnp.broadcast_to(filt[f : f + 1, :], (8, SPAN))
        row = jnp.concatenate([lane_zero, row], axis=1)
        for q in range(0, 16, 2):
            top = pltpu.roll(row, 8 * q, 1, stride=1, stride_axis=0)
            low = pltpu.roll(row, 8 * q + 8, 1, stride=1, stride_axis=0)
            toep[f, 8 * q : 8 * q + 16, :] = jnp.concatenate([top, low], axis=0).astype(BF16)

    block = lax.broadcasted_iota(jnp.int32, (PEERS, TOK), 0)
    first = jnp.zeros((PEERS, TOK), jnp.int32)
    last = jnp.full((PEERS, TOK), PEERS, jnp.int32)
    edge = jnp.int32(0)
    for genome in range(4):
        first = jnp.where(block >= edge, edge, first)
        edge = edge + (lengths[genome] >> 7)
        last = jnp.minimum(last, jnp.where(block < edge, edge, PEERS))
    before = block - first
    after = last - 1 - block

    xpad[:, 0:LAGS, :] = jnp.zeros((NFL, LAGS, TOK), F32)
    gpad[:, PEERS : PEERS + LAGS, :] = jnp.zeros((NFL, LAGS, TOK), F32)

    def convolve(part):
        unpacked[part] = recv1[part].astype(F32).reshape(PEERS * 8, TOK)
        backs = []
        for e in range(QUAD):
            f = QUAD * part + e
            xpad[f, LAGS : LAGS + PEERS, :] = unpacked[part, pl.ds(e, PEERS, stride=8), :]
            gpad[f, 0:PEERS, :] = unpacked[part, pl.ds(QUAD + e, PEERS, stride=8), :]
            left, right = [], []
            for lag in range(LAGS):
                back = jnp.where(before >= lag, xpad[f, LAGS - lag : LAGS - lag + PEERS, :], 0.0)
                ahead = jnp.where(after >= lag, gpad[f, lag : lag + PEERS, :], 0.0)
                piece = jnp.concatenate([back, ahead], axis=0).astype(BF16)
                xcat[f, :, TOK * lag : TOK * lag + TOK] = piece[0:PEERS]
                left.append(piece)
                right.append(toep[f, :, TOK * lag + TOK : TOK * lag + 2 * TOK])
            out = jnp.dot(
                jnp.concatenate(left, axis=1), jnp.concatenate(right, axis=0),
                preferred_element_type=F32,
            )
            result[part, pl.ds(e, PEERS, stride=8), :] = out[0:PEERS]
            backs.append(out[PEERS:].astype(BF16))
        back = jnp.dot(jnp.concatenate(backs, axis=0), flip, preferred_element_type=F32)
        for e in range(QUAD):
            result[part, pl.ds(QUAD + e, PEERS, stride=8), :] = back[PEERS * e : PEERS * e + PEERS]
        send2[part] = result[part].reshape(PEERS, 8, TOK).astype(BF16)

    def correlate(part):
        for e in range(QUAD):
            f = QUAD * part + e
            lhs = gpad[f, 0:PEERS, :].T.astype(BF16)
            rhs = [xcat[f, :, TOK * lag : TOK * lag + TOK] for lag in range(LAGS - 1, -1, -1)]
            cross = jnp.dot(lhs, jnp.concatenate(rhs, axis=1), preferred_element_type=F32)
            cross = jnp.concatenate([cross, jnp.zeros((TOK, TOK), F32)], axis=1)
            skew = pltpu.roll(cross[0:8], 0, 1, stride=1, stride_axis=0)
            for q in range(1, 16):
                skew = skew + pltpu.roll(cross[8 * q : 8 * q + 8], 8 * q, 1, stride=1, stride_axis=0)
            for tile in range(LAGS):
                diag[f, 8 * tile : 8 * tile + 8, :] = skew[:, TOK * tile : TOK * tile + TOK]
            total = diag[f, pl.ds(0, LAGS, stride=8), :]
            for j in range(1, 8):
                total = total + diag[f, pl.ds(j, LAGS, stride=8), :]
            sums[LAGS * f : LAGS * f + LAGS, :] = total

    def collect(half):
        for e in range(QUAD):
            f = QUAD * half + e
            gsend[half, 0, 16 * e : 16 * e + 16, :] = sums[LAGS * f + 16 : LAGS * f + 32].astype(BF16)
            gsend[half, 1, 16 * e : 16 * e + 16, :] = sums[LAGS * f : LAGS * f + 16].astype(BF16)
        for to in range(2):
            copy = pltpu.make_async_remote_copy(
                src_ref=gsend.at[half, to], dst_ref=grecv.at[half, ch],
                send_sem=gssem.at[half, to], recv_sem=grsem.at[half, ch],
                device_id=(seq, jnp.int32(to)), device_id_type=MESH,
            )
            pl.when(ch != to)(copy.start)

            @pl.when(ch == to)
            def _():
                grecv[half, pl.ds(ch, 1)] = gsend[half, to : to + 1]

    own2 = []
    for part in range(PARTS):
        finish(recv1, rsem1, part)
        own1[part].wait()
        convolve(part)
        own2.append(exchange(send2, recv2, ssem2, rsem2, part))
    for part in range(PARTS):
        correlate(part)
        collect(part)

    @pl.when(ch < 2)
    def _():
        for half in range(PARTS):
            for source in range(4):
                @pl.when(ch != source)
                def _():
                    piece = grecv.at[half, source]
                    pltpu.make_async_copy(piece, piece, grsem.at[half, source]).wait()
            sums[64 * half : 64 * half + 64, :] = jnp.dot(
                jnp.sum(grecv[half].astype(F32), axis=0),
                anti_identity(TOK, F32),
                precision=lax.Precision.HIGHEST, preferred_element_type=F32,
            )
        for tile in range(16):
            grad_filters[:, TOK * (15 - tile) : TOK * (16 - tile)] = sums[pl.ds(tile, NFL, stride=16), :]

    @pl.when(ch >= 2)
    def _():
        grad_filters[...] = jnp.zeros((NFL, 2048), F32)

    for part in range(PARTS):
        finish(recv2, rsem2, part)
        own2[part].wait()
        finish(send1, ssem1, part)
        finish(send2, ssem2, part)
        for to in range(2):
            @pl.when(ch != to)
            def _():
                piece = gsend.at[part, to]
                pltpu.make_async_copy(piece, piece, gssem.at[part, to]).wait()


def gating(recv2, gate, cot, part_filters, gated, grad_value, grad_gate, grad_filters, out1, out2, out3, sem):
    filters = pltpu.make_async_copy(part_filters, grad_filters, sem.at[3])
    filters.start()
    upper = lax.broadcasted_iota(jnp.int32, (PEERS, NFL, TOK), 1) < QUAD
    early = recv2[0].astype(F32)
    late = recv2[1].astype(F32)
    back = jnp.where(upper, pltpu.roll(early, QUAD, 1), late).reshape(PEERS * NFL, TOK)
    out1[...] = back.astype(BF16)
    store1 = pltpu.make_async_copy(out1, grad_value, sem.at[0])
    store1.start()
    conv = jnp.where(upper, early, pltpu.roll(late, QUAD, 1)).reshape(PEERS * NFL, TOK)
    out2[...] = (gate[...].astype(F32) * conv).astype(BF16)
    store2 = pltpu.make_async_copy(out2, gated, sem.at[1])
    store2.start()
    out3[...] = (cot[...].astype(F32) * conv).astype(BF16)
    store3 = pltpu.make_async_copy(out3, grad_gate, sem.at[2])
    store3.start()
    for store in (filters, store1, store2, store3):
        store.wait()


def per_device(value_in, gate_in, grad_out, filters, genome_lengths):
    shape = value_in.shape
    flat = (shape[1], shape[2])
    hbm = pl.BlockSpec(memory_space=pltpu.HBM)
    messages = pltpu.VMEM((PARTS, PEERS, 8, TOK), BF16)
    flats = [array.reshape(flat) for array in (value_in, gate_in, grad_out)]
    tail = jax.ShapeDtypeStruct((NFL, 2048), F32)
    vmem = pl.BlockSpec(memory_space=pltpu.VMEM)
    held = [
        pltpu.with_memory_space_constraint(array, pltpu.HBM)
        for array in (genome_lengths, *flats, filters)
    ]
    outs = pl.pallas_call(
        kernel,
        out_shape=[
            jax.ShapeDtypeStruct((PARTS, PEERS, 8, TOK), BF16),
            jax.ShapeDtypeStruct(flat, BF16), jax.ShapeDtypeStruct(flat, BF16), tail,
        ],
        in_specs=[hbm] * 5,
        out_specs=[vmem] * 4,
        scratch_shapes=[
            pltpu.SMEM((4,), jnp.int32),
            pltpu.VMEM(flat, BF16),
            pltpu.VMEM((NFL, SPAN), F32),
            messages, messages, messages,
            pltpu.VMEM((PARTS, PEERS * 8, TOK), F32), pltpu.VMEM((PARTS, PEERS * 8, TOK), F32),
            pltpu.VMEM((NFL, PEERS + LAGS, TOK), F32), pltpu.VMEM((NFL, PEERS + LAGS, TOK), F32),
            pltpu.VMEM((NFL, TOK, SPAN + TOK), BF16),
            pltpu.VMEM((NFL, PEERS, SPAN), BF16),
            pltpu.VMEM((NFL, 8 * LAGS, TOK), F32), pltpu.VMEM((NFL * LAGS, TOK), F32),
            pltpu.VMEM((PARTS, 2, 64, TOK), BF16), pltpu.VMEM((PARTS, 4, 64, TOK), BF16),
            pltpu.SemaphoreType.DMA((5,)),
            pltpu.SemaphoreType.DMA((PARTS,)), pltpu.SemaphoreType.DMA((PARTS,)),
            pltpu.SemaphoreType.DMA((PARTS,)), pltpu.SemaphoreType.DMA((PARTS,)),
            pltpu.SemaphoreType.DMA((PARTS, 2)), pltpu.SemaphoreType.DMA((PARTS, 4)),
            pltpu.SemaphoreType.DMA((PARTS,)),
        ],
        compiler_params=pltpu.CompilerParams(
            collective_id=0, has_side_effects=True, vmem_limit_bytes=40 * 1024 * 1024
        ),
        name="hyena",
    )(*held)
    outs = pl.pallas_call(
        gating,
        out_shape=[jax.ShapeDtypeStruct(flat, BF16)] * 3 + [tail],
        in_specs=[vmem] * 4,
        out_specs=[hbm] * 4,
        scratch_shapes=[pltpu.VMEM(flat, BF16)] * 3 + [pltpu.SemaphoreType.DMA((4,))],
        compiler_params=pltpu.CompilerParams(vmem_limit_bytes=8 * 1024 * 1024),
        name="gating",
    )(*outs)
    return (outs[0].reshape(shape), outs[1].reshape(shape), outs[2].reshape(shape), outs[3])


def solution(mesh):
    tokens = P("ch", None, "seq")
    return jax.shard_map(
        per_device,
        mesh=mesh,
        in_specs=(tokens, tokens, tokens, P("seq", None), P()),
        out_specs=(tokens, tokens, tokens, P("seq", "ch")),
        check_vma=False,
    )
```
